512 devices in a mesh: section: 8 (over y), replica: 64 (over z, x, core).
Axes of the slice: x: 4, y: 8, z: 8, core: 2. Of those that a mesh axis runs over, the one named last changes fastest.
Arguments:
- coords_in: bfloat16 [2, 8192, 512], P(None, 'replica'), may hold values from -6 to 6
- token_rows: bfloat16 [2, 8192, 2048], P(None, 'replica'), may hold values from -16 to 16
- cotangent: bfloat16 [2, 8192, 512], P(None, 'replica'), may hold values from -6 to 6
- subspace_basis: bfloat16 [512, 2048], replicated, may hold values from -0.25 to 0.25
- norm_gain: float32 [8, 2048], P('section'), may hold values from 0.5 to 1.5
- gate_weight: float32 [8, 2048, 256], P('section', 'replica'), may hold values from -0.125 to 0.125
- up_weight: bfloat16 [8, 2048, 256], P('section', 'replica'), may hold values from -0.125 to 0.125
- down_weight: float32 [8, 256, 512], P('section', 'replica'), may hold values from -0.375 to 0.375
- gate_moment: float32 [8, 2048, 256], P('section', 'replica'), may hold values from -0.625 to 0.625
- gate_second: float32 [8, 2048, 256], P('section', 'replica'), may hold values from 0.01 to 0.1
- down_moment: float32 [8, 256, 512], P('section', 'replica'), may hold values from -0.625 to 0.625
- down_second: float32 [8, 256, 512], P('section', 'replica'), may hold values from 0.01 to 0.1
Outputs:
- section_coords: bfloat16 [8, 2, 8192, 512], P('section', None, 'replica')
- coord_grads: bfloat16 [8, 2, 8192, 512], P('section', None, 'replica')
- gate_new: float32 [8, 2048, 256], P('section', 'replica')
- gate_moment_new: float32 [8, 2048, 256], P('section', 'replica')
- gate_second_new: float32 [8, 2048, 256], P('section', 'replica')
- down_new: float32 [8, 256, 512], P('section', 'replica')
- down_moment_new: float32 [8, 256, 512], P('section', 'replica')
- down_second_new: float32 [8, 256, 512], P('section', 'replica')
The draws below stay inside these ranges and needn't reach their ends.
All inputs are finite; a program needn't handle non-finite values.
Results may differ from the reference program's by a relative error of at most 0.03.
Values may be sent and summed in bfloat16 or wider, within the bound.
A program may use at most 64 MiB of HBM per device.

```python
import math
import jax
import jax.numpy as jnp
from jax import lax

D = 2048
FF = 256
K = 512
MB = 2
ROWS = 8192
TOKENS = 16384
SECTIONS = 8


def with_spikes(array, own_key, source, target, parts, factor):
    def block_of(axis_at):
        return (jnp.arange(array.shape[axis_at]) // (array.shape[axis_at] // parts)).reshape((-1,) + (1,) * (array.ndim - 1 - axis_at))

    first = jax.random.permutation(own_key, parts)[block_of(target)]
    far = (block_of(target) + parts // 2) % parts
    return jnp.where((block_of(source) == first) | (block_of(source) == far), factor * array, array)


def block_scale(rng, extent, cuts, smallest, top_value):
    level, own = 1.0, jax.random.fold_in(rng, 6)
    for position, parts in cuts:
        heights = jnp.exp(jax.random.uniform(jax.random.fold_in(own, position), (parts,), jnp.float32, smallest / len(cuts), top_value / len(cuts)))
        level = level * jnp.repeat(heights, extent[position] // parts).reshape([-1 if axis == position else 1 for axis in range(len(extent))])
    return level


def gaussian(rng, extent, deviation, most, pieces=(), held_as=jnp.bfloat16):
    factor_of = block_scale(rng, extent, pieces, -0.22, 0.18) if pieces else 1.0
    result = jax.random.normal(rng, extent, jnp.float32) * deviation * factor_of
    return jnp.minimum(jnp.maximum(result, -most), most).astype(held_as)


def gaussian_with(stream_key, dims, scale, limit, pieces, heavy, kind=jnp.bfloat16):
    entries = scale * jax.random.normal(stream_key, dims, jnp.float32)
    if pieces:
        entries = entries * block_scale(stream_key, dims, pieces, -0.22, 0.18)
    return jnp.clip(with_spikes(entries, jax.random.fold_in(stream_key, 3), *heavy), -limit, limit).astype(kind)


def setup_inputs(seed: int = 0) -> dict:
    splits = jax.random.split(jax.random.key(seed), 13)
    coords_in = gaussian(splits[0], (MB, ROWS, K), 1.0, 6.0, ((1, 64),))
    token_rows = gaussian_with(splits[1], (MB, ROWS, D), 1.0, 16.0, ((1, 64),), (1, 2, 64, 4.0))
    cotangent = gaussian(splits[2], (MB, ROWS, K), 1.0, 6.0, ((1, 64),))
    subspace_basis = gaussian(splits[3], (K, D), K ** -0.5, 0.25)
    norm_gain = jnp.clip(0.5 + 1.0 * jax.random.uniform(splits[4], (SECTIONS, D), jnp.float32) ** block_scale(splits[4], (SECTIONS, D), ((0, 8),), -0.2, 0.2), 0.5, 1.5)
    gate_weight = gaussian(splits[5], (SECTIONS, D, FF), D ** -0.5, 0.125, ((0, 8), (1, 64)), jnp.float32)
    up_weight = gaussian(splits[6], (SECTIONS, D, FF), D ** -0.5, 0.125, ((0, 8), (1, 64)))
    down_weight = gaussian(splits[7], (SECTIONS, FF, K), FF ** -0.5, 0.375, ((0, 8), (1, 64)), jnp.float32)
    gate_moment = gaussian(splits[8], (SECTIONS, D, FF), 0.1, 0.625, ((0, 8), (1, 64)), jnp.float32)
    gate_second = jnp.clip(jnp.exp(math.log(0.1) - 2.3025851 * jax.random.uniform(splits[9], (SECTIONS, D, FF), jnp.float32) ** block_scale(splits[9], (SECTIONS, D, FF), ((0, 8), (1, 64)), -0.2, 0.2)), 0.01, 0.1)
    down_moment = gaussian(splits[10], (SECTIONS, FF, K), 0.1, 0.625, ((0, 8), (1, 64)), jnp.float32)
    down_second = jnp.clip(jnp.exp(math.log(0.1) - 2.3025851 * jax.random.uniform(splits[11], (SECTIONS, FF, K), jnp.float32) ** block_scale(splits[11], (SECTIONS, FF, K), ((0, 8), (1, 64)), -0.2, 0.2)), 0.01, 0.1)
    return {"coords_in": coords_in, "token_rows": token_rows, "cotangent": cotangent, "subspace_basis": subspace_basis, "norm_gain": norm_gain, "gate_weight": gate_weight, "up_weight": up_weight, "down_weight": down_weight, "gate_moment": gate_moment, "gate_second": gate_second, "down_moment": down_moment, "down_second": down_second}


epsilon = 1e-06
learn_rate = 0.001
decay_first = 0.9
decay_second = 0.95
step_count = 10
adam_floor = 1e-08

def contract_last(left, right):
    return lax.dot_general(left, right, (((1,), (1,)), ((), ())), preferred_element_type=jnp.float32)

def contract_first(left, right):
    return lax.dot_general(left, right, (((0,), (0,)), ((), ())), preferred_element_type=jnp.float32)

def silu_parts(gate_value):
    sigma = jax.nn.sigmoid(gate_value)
    return (gate_value * sigma, sigma * (1.0 + gate_value * (1.0 - sigma)))

def section_forward(coords, token_block, subspace_basis, gain_row, w_gate, w_up, w_down):
    expanded = jnp.dot(coords, subspace_basis, preferred_element_type=jnp.float32) + token_block.astype(jnp.float32)
    inverse = lax.rsqrt(lax.optimization_barrier(jnp.mean(expanded * expanded, axis=1, keepdims=True)) + epsilon)
    normed = (expanded * inverse * gain_row).astype(jnp.bfloat16)
    gate_value = jnp.dot(normed, w_gate, preferred_element_type=jnp.float32)
    up_value = jnp.dot(normed, w_up, preferred_element_type=jnp.float32)
    active, slope_value = silu_parts(gate_value)
    hidden = (active * up_value).astype(jnp.bfloat16)
    output = (coords.astype(jnp.float32) + jnp.dot(hidden, w_down, preferred_element_type=jnp.float32)).astype(jnp.bfloat16)
    return (output, (expanded, inverse, normed, gate_value, up_value, hidden))

def section_backward(next_grad, saved, subspace_basis, gain_row, w_gate, w_up, w_down):
    expanded, inverse, normed, gate_value, up_value, hidden = saved
    hidden_grad = contract_last(next_grad, w_down)
    down_term = contract_first(hidden, next_grad)
    active, slope_value = silu_parts(gate_value)
    gate_grad = (hidden_grad * up_value * slope_value).astype(jnp.bfloat16)
    up_grad = (hidden_grad * active).astype(jnp.bfloat16)
    gate_term = contract_first(normed, gate_grad)
    normed_grad = contract_last(gate_grad, w_gate) + contract_last(up_grad, w_up)
    scaled = normed_grad * gain_row
    centred = expanded * inverse
    expanded_grad = (inverse * (scaled - centred * lax.optimization_barrier(jnp.mean(scaled * centred, axis=1, keepdims=True)))).astype(jnp.bfloat16)
    coord_grad = (next_grad.astype(jnp.float32) + contract_last(expanded_grad, subspace_basis)).astype(jnp.bfloat16)
    return (coord_grad, gate_term, down_term)

def adam_update(weight_now, moment, second, gradient):
    moment_new = decay_first * moment + (1.0 - decay_first) * gradient
    second_new = decay_second * second + (1.0 - decay_second) * gradient * gradient
    update = learn_rate * (moment_new / (1.0 - decay_first ** step_count)) / (jnp.sqrt(second_new / (1.0 - decay_second ** step_count)) + adam_floor)
    return (weight_now - update, moment_new, second_new)

def reference(coords_in, token_rows, cotangent, subspace_basis, norm_gain, gate_weight, up_weight, down_weight, gate_moment, gate_second, down_moment, down_second):
    gate_low = gate_weight.astype(jnp.bfloat16)
    down_low = down_weight.astype(jnp.bfloat16)
    layer_inputs = []
    layer_outputs = []
    current = coords_in
    for layer_index in range(SECTIONS):
        layer_inputs.append(current)
        weights = (subspace_basis, norm_gain[layer_index][None, :], gate_low[layer_index], up_weight[layer_index], down_low[layer_index])
        results = [section_forward(current[batch_index], token_rows[batch_index], *weights)[0] for batch_index in range(MB)]
        current = jnp.stack(results)
        layer_outputs.append(current)
    section_coords = jnp.stack(layer_outputs)
    grad_scale = 1.0 / math.sqrt(TOKENS)
    next_grads = cotangent
    back_list = [None] * SECTIONS
    gate_parts = [None] * SECTIONS
    down_parts = [None] * SECTIONS
    for layer_index in range(SECTIONS - 1, -1, -1):
        weights = (subspace_basis, norm_gain[layer_index][None, :], gate_low[layer_index], up_weight[layer_index], down_low[layer_index])
        coord_list = []
        gate_total = jnp.zeros((D, FF), jnp.float32)
        down_total = jnp.zeros((FF, K), jnp.float32)
        for batch_index in range(MB):
            saved = section_forward(layer_inputs[layer_index][batch_index], token_rows[batch_index], *weights)[1]
            coord_grad, gate_term, down_term = section_backward(next_grads[batch_index], saved, *weights)
            coord_list.append(coord_grad)
            gate_total = gate_total + gate_term
            down_total = down_total + down_term
        next_grads = jnp.stack(coord_list)
        back_list[layer_index] = next_grads
        gate_parts[layer_index] = adam_update(gate_weight[layer_index], gate_moment[layer_index], gate_second[layer_index], gate_total * grad_scale)
        down_parts[layer_index] = adam_update(down_weight[layer_index], down_moment[layer_index], down_second[layer_index], down_total * grad_scale)
    coord_grads = jnp.stack(back_list)
    gate_new = jnp.stack([item[0] for item in gate_parts])
    gate_moment_new = jnp.stack([item[1] for item in gate_parts])
    gate_second_new = jnp.stack([item[2] for item in gate_parts])
    down_new = jnp.stack([item[0] for item in down_parts])
    down_moment_new = jnp.stack([item[1] for item in down_parts])
    down_second_new = jnp.stack([item[2] for item in down_parts])
    return (section_coords, coord_grads, gate_new, gate_moment_new, gate_second_new, down_new, down_moment_new, down_second_new)
```

```python
import math

import jax
import jax.numpy as jnp
from jax import lax
from jax.experimental import pallas as pl
from jax.experimental.pallas import tpu as pltpu
from jax.sharding import PartitionSpec as P

F32 = jnp.float32
BF16 = jnp.bfloat16
MESH = pl.DeviceIdType.MESH
epsilon = 1e-06
learn_rate = 0.001
decay_first = 0.9
decay_second = 0.95
step_count = 10
adam_floor = 1e-08

D, FF, K = 2048, 256, 512
ROWS = 256
PIECE = 32
PIECES = ROWS // PIECE
NZ, NX, NS = 8, 4, 8
CHUNK = D // NZ
GATHER_ROWS = 80
REDUCE_ROWS = 48
Z_ORDER = (1, 7, 2, 6, 3, 5, 4)


def dot_last(left, right):
    return lax.dot_general(left, right, (((1,), (1,)), ((), ())), preferred_element_type=F32)


def dot(left, right):
    return jnp.dot(left, right, preferred_element_type=F32)


def adam_update(weight_now, moment, second, gradient):
    moment_new = decay_first * moment + (1.0 - decay_first) * gradient
    second_new = decay_second * second + (1.0 - decay_second) * gradient * gradient
    update = (
        learn_rate
        * (moment_new / (1.0 - decay_first**step_count))
        / (jnp.sqrt(second_new / (1.0 - decay_second**step_count)) + adam_floor)
    )
    return (weight_now - update, moment_new, second_new)


def kernel(
    coords_hbm, tok_hbm, cot_hbm, basis_hbm, gain, gate_w, up_w, down_w, gate_m, gate_s, down_m, down_s,
    o_coords, o_grads, o_gw, o_gm, o_gs, o_dw, o_dm, o_ds,
    tok, basis, cin, gin, wbuf, lhs, acc_gp, acc_mt, mg, mt, wd, wdt, tok_sq, inv_s, gate_v, up_v, act_s, slope_s,
    e_s, hid, gg_s, norm_t, wide, narrow, stage, gsend, gcore, xsum, xrecv, zsum, zrecv,
    local_sem, az_s, az_r, ax_s, ax_r, ac_s, ac_r, f_s, f_r, b_s, b_r, rc_s, rc_r, rx_s, rx_r, rz_s, rz_r,
):
    s = lax.axis_index("section")
    r = lax.axis_index("replica")
    z = r // 8
    x = lax.rem(r // 2, 4)
    c = lax.rem(r, 2)

    def device(z_of, x_of, c_of):
        return (s, (z_of * 4 + x_of) * 2 + c_of)

    def z_at(k):
        return lax.rem(z + k + NZ, NZ)

    def x_at(k):
        return lax.rem(x + k + NX, NX)

    partner = device(z, x, 1 - c)

    def remote(source, target, send_sem, recv_sem, where):
        return pltpu.make_async_remote_copy(
            src_ref=source, dst_ref=target, send_sem=send_sem, recv_sem=recv_sem,
            device_id=where, device_id_type=MESH,
        )

    load_tok = pltpu.make_async_copy(tok_hbm, tok, local_sem.at[0])
    load_basis = pltpu.make_async_copy(basis_hbm, basis, local_sem.at[1])
    load_basis.start()
    load_tok.start()

    barrier = pltpu.get_barrier_semaphore()
    for k in range(1, NZ):
        pl.semaphore_signal(barrier, inc=1, device_id=device(z_at(k), x, c), device_id_type=MESH)
    for k in range(1, NX):
        pl.semaphore_signal(barrier, inc=1, device_id=device(z, x_at(k), c), device_id_type=MESH)
    pl.semaphore_signal(barrier, inc=1, device_id=partner, device_id_type=MESH)
    for k in (1, NS - 1):
        pl.semaphore_signal(barrier, inc=1, device_id=(lax.rem(s + k, NS), r), device_id_type=MESH)

    stage[...] = jnp.zeros_like(stage)
    for p in range(2):
        stage[4 * p : 4 * p + 4, :] = down_w[:, 256 * p : 256 * p + 256]
    wbuf[z, x, c, 0:32, :] = gate_w[...].astype(BF16)
    wbuf[z, x, c, 32:64, :] = up_w[...]
    wbuf[z, x, c, 64:80, :] = stage[...].astype(BF16)

    pl.semaphore_wait(barrier, NZ - 1 + NX - 1 + 1 + 2)

    def gather_z(k):
        return remote(wbuf.at[z, x, c], wbuf.at[z, x, c], az_s.at[k - 1], az_r.at[k - 1], device(z_at(k), x, c))

    def gather_x(j, k):
        block = wbuf.at[z_at(-j), x, c]
        return remote(block, block, ax_s.at[j, k - 1], ax_r.at[j, k - 1], device(z, x_at(k), c))

    def gather_c(j):
        block = wbuf.at[z_at(-j), pl.ds(0, NX), c]
        return remote(block, block, ac_s.at[j], ac_r.at[j], partner)

    for k in Z_ORDER:
        gather_z(k).start()
    for k in range(1, NX):
        gather_x(0, k).start()

    load_basis.wait()
    load_tok.wait()
    acc_gp[...] = jnp.zeros_like(acc_gp)
    square = jnp.zeros((ROWS, 1), F32)
    for j in range(NZ):
        cols = slice(CHUNK * j, CHUNK * (j + 1))
        b_now = basis[:, cols]
        t_now = tok[:, cols]
        acc_gp[0:K, :] += dot_last(b_now, b_now)
        acc_gp[K:, :] += dot_last(t_now, b_now)
        t32 = t_now.astype(F32)
        square = square + jnp.sum(t32 * t32, axis=1, keepdims=True)
        lhs[j, 0:K, :] = (b_now.astype(F32) * gain[:, cols]).astype(BF16)
        lhs[j, K:, :] = (t32 * gain[:, cols]).astype(BF16)
    tok_sq[...] = jnp.broadcast_to(square, tok_sq.shape)
    mg[:, K:] = acc_gp[0:K, :].astype(BF16)
    acc_mt[...] = jnp.zeros_like(acc_mt)

    for k in Z_ORDER:
        gather_z(k).wait_recv()
        for m in range(1, NX):
            gather_x(k, m).start()
    for j in (0,) + Z_ORDER:
        for m in range(1, NX):
            gather_x(j, m).wait_recv()
        gather_c(j).start()
    for j in (0,) + Z_ORDER:
        gather_c(j).wait_recv()
        at = z_at(-j)
        left = lhs[at]
        acc_mt[:, 0:FF] += dot(left, wbuf[at, :, :, 0:32, :].reshape(CHUNK, FF))
        acc_mt[:, FF:] += dot(left, wbuf[at, :, :, 32:64, :].reshape(CHUNK, FF))
    mg[:, 0:K] = acc_mt[0:K, :].astype(BF16)
    for h in range(2):
        wide[h] = wbuf[:, :, :, 64:80, 128 * h : 128 * h + 128].astype(F32).reshape(1024, 128)
    for p in range(2):
        for h in range(2):
            for i in range(4):
                narrow[2 * p + h, pl.ds(i, 64, stride=4), :] = wide[h, pl.ds(4 * p + i, 64, stride=16), :]
    for q in range(4):
        wd[:, 128 * q : 128 * q + 128] = narrow[q].astype(BF16)

    @pl.when(s == 0)
    def _():
        copy = pltpu.make_async_copy(coords_hbm, cin, local_sem.at[2])
        copy.start()
        copy.wait()

    @pl.when(s == NS - 1)
    def _():
        copy = pltpu.make_async_copy(cot_hbm, gin, local_sem.at[3])
        copy.start()
        copy.wait()

    def rows_of(i):
        return pl.ds(pl.multiple_of(i * PIECE, PIECE), PIECE)

    def relay_forward(i):
        return remote(o_coords.at[rows_of(i)], cin.at[rows_of(i)], f_s.at[i], f_r.at[i], (lax.rem(s + 1, NS), r))

    def relay_backward(i):
        return remote(o_grads.at[rows_of(i)], gin.at[rows_of(i)], b_s.at[i], b_r.at[i], (lax.rem(s + NS - 1, NS), r))

    def forward(i):
        rows = rows_of(i)

        @pl.when(s > 0)
        def _():
            relay_forward(i).wait_recv()

        now = cin[rows, :]
        now32 = now.astype(F32)
        product = dot(now, mg[...])
        side = acc_gp[pl.ds(pl.multiple_of(K + i * PIECE, PIECE), PIECE), :]
        e_now = product[:, K:] + side
        total = jnp.sum(now32 * (e_now + side), axis=1, keepdims=True) + tok_sq[rows, 0:1]
        inverse = lax.rsqrt(jnp.maximum(total, 0.0) * (1.0 / D) + epsilon)
        both = inverse * (product[:, 0:K] + acc_mt[pl.ds(pl.multiple_of(K + i * PIECE, PIECE), PIECE), :])
        gate_value = both[:, 0:FF]
        up_value = both[:, FF:]
        sigma = jax.nn.sigmoid(gate_value)
        active = gate_value * sigma
        hidden = (active * up_value).astype(BF16)
        o_coords[rows, :] = (now32 + dot(hidden, wd[...])).astype(BF16)

        @pl.when(s < NS - 1)
        def _():
            relay_forward(i).start()

        hid[rows, :] = hidden
        inv_s[rows, :] = jnp.broadcast_to(inverse, (PIECE, 128))
        gate_v[rows, :] = gate_value
        up_v[rows, :] = up_value
        act_s[rows, :] = active
        slope_s[rows, :] = up_value * (sigma * (1.0 + gate_value * (1.0 - sigma)))
        e_s[rows, :] = e_now

    def backward(i):
        rows = rows_of(i)

        @pl.when(s < NS - 1)
        def _():
            relay_backward(i).wait_recv()

        now = gin[rows, :]
        hidden_grad = dot(now, wdt[...])
        gate_grad = (hidden_grad * slope_s[rows, :]).astype(BF16)
        up_grad = (hidden_grad * act_s[rows, :]).astype(BF16)
        inverse = inv_s[rows, 0:1]
        back = dot(gate_grad, mt[0:FF, :]) + dot(up_grad, mt[FF:, :])
        shared = jnp.sum(
            gate_grad.astype(F32) * gate_v[rows, :] + up_grad.astype(F32) * up_v[rows, :], axis=1, keepdims=True
        ) * (1.0 / D)
        o_grads[rows, :] = (now.astype(F32) + inverse * (back - (shared * inverse) * e_s[rows, :])).astype(BF16)

        @pl.when(s > 0)
        def _():
            relay_backward(i).start()

        gg_s[rows, :] = gate_grad

    def transposed():
        mt[...] = acc_mt[0:K, :].T.astype(BF16)
        wdt[...] = wd[...].astype(F32).T.astype(BF16)

    def normed():
        for j in range(NZ):
            cols = slice(CHUNK * j, CHUNK * (j + 1))
            value = dot(cin[...], basis[:, cols]) + tok[:, cols].astype(F32)
            value = value * inv_s[:, 0:1] * gain[:, cols]
            norm_t[j] = value.T.astype(BF16)

    first, last = s == 0, s == NS - 1

    def step(k, carry):
        is_prep = jnp.where(first, k == PIECES, k == 0)
        is_norm = jnp.where(last, k == 2 * PIECES + 1, k == PIECES + 1)
        is_f = jnp.where(
            first, k < PIECES,
            jnp.where(last, (lax.rem(k, 2) == 1) & (k < 2 * PIECES + 1), (k >= 1) & (k <= PIECES)),
        )
        f_at = jnp.where(first, k, jnp.where(last, (k - 1) // 2, k - 1))
        is_b = jnp.where(last, (lax.rem(k, 2) == 0) & (k >= 2), k >= PIECES + 2)
        b_at = jnp.where(last, (k - 2) // 2, k - PIECES - 2)

        @pl.when(is_prep)
        def _():
            transposed()

        @pl.when(is_f)
        def _():
            forward(f_at)

        @pl.when(is_norm)
        def _():
            normed()

        @pl.when(is_b)
        def _():
            backward(b_at)

        return carry

    lax.fori_loop(0, 2 * PIECES + 2, step, 0)

    down_sum = dot(hid[...].astype(F32).T.astype(BF16), gin[...])
    for q in range(4):
        narrow[q] = down_sum[:, 128 * q : 128 * q + 128]
    wide[...] = jnp.zeros_like(wide)
    for p in range(2):
        for h in range(2):
            for i in range(4):
                wide[h, pl.ds(4 * p + i, 64, stride=16), :] = narrow[2 * p + h, pl.ds(i, 64, stride=4), :]
    for h in range(2):
        gsend[:, :, :, 32:48, 128 * h : 128 * h + 128] = wide[h].reshape(NZ, NX, 2, 16, 128).astype(BF16)

    def reduce_c(j):
        at = z_at(j)
        return remote(gsend.at[at, pl.ds(0, NX), 1 - c], gcore.at[at], rc_s.at[j], rc_r.at[j], partner)

    def reduce_x(j, k):
        at = z_at(j)
        return remote(xsum.at[at, x_at(k)], xrecv.at[at, k - 1], rx_s.at[j, k - 1], rx_r.at[j, k - 1], device(z, x_at(k), c))

    def reduce_z(j):
        at = z_at(j)
        return remote(zsum.at[at], zrecv.at[j - 1], rz_s.at[j - 1], rz_r.at[j - 1], device(at, x, c))

    far_first = Z_ORDER[::-1] + (0,)
    for j in far_first:
        at = z_at(j)
        part = dot(norm_t[at], gg_s[...])
        gsend[at, :, :, 0:32, :] = part.reshape(NX, 2, 32, FF).astype(BF16)
        reduce_c(j).start()
    for j in far_first:
        at = z_at(j)
        reduce_c(j).wait_recv()
        xsum[at] = (gsend[at, :, c].astype(F32) + gcore[at].astype(F32)).astype(BF16)
        for k in range(1, NX):
            reduce_x(j, k).start()
    for j in far_first:
        at = z_at(j)
        total = xsum[at, x].astype(F32)
        for k in range(1, NX):
            reduce_x(j, k).wait_recv()
            total = total + xrecv[at, k - 1].astype(F32)
        if j == 0:
            own = total
        else:
            zsum[at] = total.astype(BF16)
            reduce_z(j).start()
    for j in Z_ORDER:
        reduce_z(j).wait_recv()
        own = own + zrecv[j - 1].astype(F32)

    own = own * (1.0 / math.sqrt(ROWS * 64))
    o_gw[...], o_gm[...], o_gs[...] = adam_update(gate_w[...], gate_m[...], gate_s[...], own[0:32, :])
    stage[...] = own[32:48, :]
    for p in range(2):
        half = slice(256 * p, 256 * p + 256)
        o_dw[:, half], o_dm[:, half], o_ds[:, half] = adam_update(
            down_w[:, half], down_m[:, half], down_s[:, half], stage[4 * p : 4 * p + 4, :]
        )

    for k in range(1, NZ):
        gather_z(k).wait_send()
        reduce_z(k).wait_send()
    for j in range(NZ):
        gather_c(j).wait_send()
        reduce_c(j).wait_send()
        for k in range(1, NX):
            gather_x(j, k).wait_send()
            reduce_x(j, k).wait_send()

    def left(i, carry):
        @pl.when(s < NS - 1)
        def _():
            relay_forward(i).wait_send()

        @pl.when(s > 0)
        def _():
            relay_backward(i).wait_send()

        return carry

    lax.fori_loop(0, PIECES, left, 0)


def per_device(
    coords_in, token_rows, cotangent, subspace_basis, norm_gain, gate_weight, up_weight, down_weight,
    gate_moment, gate_second, down_moment, down_second,
):
    dma = pltpu.SemaphoreType.DMA
    vmem = pltpu.VMEM
    whole = pl.BlockSpec(memory_space=pltpu.VMEM)
    left = pl.BlockSpec(memory_space=pl.ANY)
    outs = pl.pallas_call(
        kernel,
        name="training_step",
        out_shape=(
            jax.ShapeDtypeStruct((ROWS, K), BF16),
            jax.ShapeDtypeStruct((ROWS, K), BF16),
            jax.ShapeDtypeStruct((32, FF), F32),
            jax.ShapeDtypeStruct((32, FF), F32),
            jax.ShapeDtypeStruct((32, FF), F32),
            jax.ShapeDtypeStruct((4, K), F32),
            jax.ShapeDtypeStruct((4, K), F32),
            jax.ShapeDtypeStruct((4, K), F32),
        ),
        in_specs=[left, left, left, left] + [whole] * 8,
        out_specs=(whole,) * 8,
        scratch_shapes=[
            vmem((ROWS, D), BF16),
            vmem((K, D), BF16),
            vmem((ROWS, K), BF16),
            vmem((ROWS, K), BF16),
            vmem((NZ, NX, 2, GATHER_ROWS, FF), BF16),
            vmem((NZ, K + ROWS, CHUNK), BF16),
            vmem((K + ROWS, K), F32),
            vmem((K + ROWS, K), F32),
            vmem((K, 2 * K), BF16),
            vmem((K, K), BF16),
            vmem((FF, K), BF16),
            vmem((K, FF), BF16),
            vmem((ROWS, 128), F32),
            vmem((ROWS, 128), F32),
            vmem((ROWS, FF), F32),
            vmem((ROWS, FF), F32),
            vmem((ROWS, FF), F32),
            vmem((ROWS, FF), F32),
            vmem((ROWS, K), F32),
            vmem((ROWS, FF), BF16),
            vmem((ROWS, FF), BF16),
            vmem((NZ, CHUNK, ROWS), BF16),
            vmem((2, 1024, 128), F32),
            vmem((4, FF, 128), F32),
            vmem((16, FF), F32),
            vmem((NZ, NX, 2, REDUCE_ROWS, FF), BF16),
            vmem((NZ, NX, REDUCE_ROWS, FF), BF16),
            vmem((NZ, NX, REDUCE_ROWS, FF), BF16),
            vmem((NZ, NX - 1, REDUCE_ROWS, FF), BF16),
            vmem((NZ, REDUCE_ROWS, FF), BF16),
            vmem((NZ - 1, REDUCE_ROWS, FF), BF16),
            dma((4,)),
            dma((NZ - 1,)), dma((NZ - 1,)),
            dma((NZ, NX - 1)), dma((NZ, NX - 1)),
            dma((NZ,)), dma((NZ,)),
            dma((PIECES,)), dma((PIECES,)),
            dma((PIECES,)), dma((PIECES,)),
            dma((NZ,)), dma((NZ,)),
            dma((NZ, NX - 1)), dma((NZ, NX - 1)),
            dma((NZ - 1,)), dma((NZ - 1,)),
        ],
        compiler_params=pltpu.CompilerParams(
            collective_id=0, has_side_effects=True, vmem_limit_bytes=48 * 1024 * 1024
        ),
        cost_estimate=pl.CostEstimate(flops=4 * 10**9, bytes_accessed=6 * 10**6, transcendentals=10**5),
    )(
        coords_in.reshape(ROWS, K), token_rows.reshape(ROWS, D), cotangent.reshape(ROWS, K), subspace_basis, norm_gain,
        gate_weight[0], up_weight[0], down_weight[0], gate_moment[0], gate_second[0], down_moment[0], down_second[0],
    )
    return (outs[0].reshape(1, 2, ROWS // 2, K), outs[1].reshape(1, 2, ROWS // 2, K)) + tuple(o[None] for o in outs[2:])


def solution(mesh):
    by_rows = P(None, "replica", None)
    by_weight = P("section", "replica", None)
    placed = (by_rows, by_rows, by_rows, P(), P("section", None)) + (by_weight,) * 7
    coords = P("section", None, "replica", None)
    return jax.shard_map(
        per_device, mesh=mesh, in_specs=placed, out_specs=(coords, coords) + (by_weight,) * 6, check_vma=False
    )
```
